32 devices in a mesh: head: 2 (over x), ctx: 16 (over z, y, core).
Axes of the slice: x: 2, y: 2, z: 4, core: 2. Of those that a mesh axis runs over, the one named last changes fastest.
Arguments:
- query_bits: int32 [256, 4096], P('head', 'ctx'), may hold values from 0 to 65535
- key_bits: int32 [256, 4096], P('head', 'ctx'), may hold values from 0 to 65535
- values: bfloat16 [4096, 4096], P('ctx', 'head'), may hold values from -6 to 6
- grad_out: bfloat16 [16, 256, 4096], P('ctx', 'head'), may hold values from -6 to 6
- tile_mask: int32 [16, 2, 2], P('ctx'), may hold values 0 or 1
Outputs:
- query_grad: bfloat16 [4096, 4096], P('ctx', 'head')
- key_grad: bfloat16 [4096, 4096], P('ctx', 'head')
- value_grad: bfloat16 [4096, 4096], P('ctx', 'head')
The draws below stay inside these ranges and needn't reach their ends.
All inputs are finite; a program needn't handle non-finite values. No bound on the sum of `tile_mask` on one device may be relied on, other than what follows from the above.
Results may differ from the reference program's by a relative error of at most 0.0049.
Values may be sent and summed in bfloat16 or wider, within the bound.
A program may use at most 128 MiB of HBM per device.

```python
import math
import jax
import jax.numpy as jnp
from jax import lax

HEADS = 32
HD = 128
TILE = 128
TOK_DEV = 256
D = 4096
WORDS = 8
TB = 2
STRETCHES = 16
TOKENS = 4096


def set_ends(result, key, smallest, high):
    index_at = [jax.random.randint(jax.random.fold_in(key, axis), (), 0, length) for axis, length in enumerate(result.shape)]
    widest = result.shape.index(max(result.shape))
    beside = index_at[:widest] + [(index_at[widest] + 1) % result.shape[widest]] + index_at[widest + 1:]
    return result.at[tuple(index_at)].set(smallest).at[tuple(beside)].set(high)


def block_levels(rng, shape, split, least, high):
    factor_of = 1.0
    for dim, shards_of in split:
        steps = jax.random.uniform(jax.random.fold_in(jax.random.fold_in(rng, 6), dim), (shards_of,), jnp.float32, least / len(split), high / len(split))
        factor_of = factor_of * jnp.repeat(jnp.exp(steps), shape[dim] // shards_of).reshape((-1,) + (1,) * (len(shape) - 1 - dim))
    return factor_of


def scatter_about(key, dims, width, limit, pieces=(), kind=jnp.bfloat16):
    drawn = jax.random.normal(key, dims, jnp.float32) * width
    if len(pieces) > 0:
        drawn = block_levels(key, dims, pieces, -0.22, 0.18) * drawn
    return jnp.clip(drawn, min=-limit, max=limit).astype(kind)


def setup_inputs(seed: int = 0) -> dict:
    key_of = jax.random.split(jax.random.key(seed), 6)
    query_bits = set_ends(jax.random.randint(key_of[0], (HEADS * WORDS, TOKENS), 0, 65536), jax.random.fold_in(key_of[0], 1), 0, 65535).astype(jnp.int32)
    key_bits = set_ends(jax.random.randint(key_of[1], (HEADS * WORDS, TOKENS), 0, 65536), jax.random.fold_in(key_of[1], 1), 0, 65535).astype(jnp.int32)
    values = scatter_about(key_of[2], (TOKENS, D), 1.0, 6.0, ((0, 16), (1, 2)))
    grad_out = scatter_about(key_of[3], (STRETCHES, TOK_DEV, D), 1.0, 6.0, ((0, 16), (1, 2)))
    tile_mask = set_ends((jax.random.randint(key_of[4], (STRETCHES, TB, TB), 0, 2) < 1).astype(jnp.int32), jax.random.fold_in(key_of[4], 1), 0, 1)
    return dict(query_bits=query_bits, key_bits=key_bits, values=values, grad_out=grad_out, tile_mask=tile_mask)


def unpack_bits(packed, heads_here):
    shifts = jnp.arange(16, dtype=jnp.int32).reshape(1, 1, 16, 1)
    spread = jnp.right_shift(packed.reshape(heads_here, -1, 1, packed.shape[-1]), shifts)
    return jnp.bitwise_and(spread, 1).astype(jnp.bfloat16).reshape(heads_here, -1, packed.shape[-1])

def token_mask(tiles, tile_size):
    tile_count = tiles.shape[0]
    tile_index = jnp.arange(tile_count, dtype=jnp.int32)
    lower = tile_index[:, None] > tile_index[None, :]
    diagonal = tile_index[:, None] == tile_index[None, :]
    allowed = jnp.where(diagonal, 1.0, jnp.where(lower, tiles.astype(jnp.float32), 0.0)).astype(jnp.float32)
    span_width = tile_count * tile_size
    expanded = jnp.broadcast_to(allowed[:, None, :, None], (tile_count, tile_size, tile_count, tile_size)).reshape(span_width, span_width)
    position = jnp.arange(span_width, dtype=jnp.int32)
    return jnp.where(position[:, None] >= position[None, :], expanded, 0.0).astype(jnp.float32)

def stretch_grads(query_spk, key_spk, value_rows, grad_rows, state, adjoint, keep_mask, att_scale):
    pair_dots = jnp.dot(grad_rows, value_rows.T, preferred_element_type=jnp.float32)
    grad_weights = (att_scale * pair_dots * keep_mask).astype(jnp.bfloat16)
    spike_dots = jnp.dot(query_spk.T, key_spk, preferred_element_type=jnp.float32)
    att_weights = (att_scale * spike_dots * keep_mask).astype(jnp.bfloat16)
    query_grad = jnp.dot(grad_weights, key_spk.T, preferred_element_type=jnp.float32) + att_scale * jnp.dot(grad_rows, state.T, preferred_element_type=jnp.float32)
    key_grad = jnp.dot(grad_weights.T, query_spk.T, preferred_element_type=jnp.float32) + att_scale * jnp.dot(value_rows, adjoint.T, preferred_element_type=jnp.float32)
    value_grad = jnp.dot(att_weights.T, grad_rows, preferred_element_type=jnp.float32) + att_scale * jnp.dot(key_spk.T, adjoint, preferred_element_type=jnp.float32)
    return (query_grad.astype(jnp.bfloat16), key_grad.astype(jnp.bfloat16), value_grad.astype(jnp.bfloat16))

def reference(query_bits, key_bits, values, grad_out, tile_mask):
    att_scale = 4.0 / (HD * math.sqrt(TOKENS))
    query_all = query_bits.reshape(HEADS, WORDS, TOKENS)
    key_all = key_bits.reshape(HEADS, WORDS, TOKENS)
    value_all = values.reshape(TOKENS, HEADS, HD).transpose(1, 0, 2)
    grad_all = grad_out.reshape(TOKENS, HEADS, HD).transpose(1, 0, 2)

    def one_head(head_item):
        query_words, key_words, value_head, grad_head = head_item
        query_spk = unpack_bits(query_words, 1)[0].reshape(HD, STRETCHES, TOK_DEV).transpose(1, 0, 2)
        key_spk = unpack_bits(key_words, 1)[0].reshape(HD, STRETCHES, TOK_DEV).transpose(1, 0, 2)
        value_stretches = value_head.reshape(STRETCHES, TOK_DEV, HD)
        grad_stretches = grad_head.reshape(STRETCHES, TOK_DEV, HD)
        state_terms = jnp.einsum('cdt,cte->cde', key_spk.astype(jnp.float32), value_stretches.astype(jnp.float32))
        adjoint_terms = jnp.einsum('cdt,cte->cde', query_spk.astype(jnp.float32), grad_stretches.astype(jnp.float32))
        zero_block = jnp.zeros((1, HD, HD), jnp.float32)
        states = jnp.concatenate([zero_block, jnp.cumsum(state_terms, axis=0)[:-1]], axis=0).astype(jnp.bfloat16)
        adjoints = jnp.concatenate([jnp.cumsum(adjoint_terms[::-1], axis=0)[::-1][1:], zero_block], axis=0).astype(jnp.bfloat16)

        def one_stretch(stretch_item):
            stretch_query, stretch_key, stretch_value, stretch_grad, stretch_state, stretch_adjoint, stretch_tiles = stretch_item
            return stretch_grads(stretch_query, stretch_key, stretch_value, stretch_grad, stretch_state, stretch_adjoint, token_mask(stretch_tiles, TILE), att_scale)
        grads_query, grads_key, grads_value = lax.map(one_stretch, (query_spk, key_spk, value_stretches, grad_stretches, states, adjoints, tile_mask))
        return (grads_query.reshape(TOKENS, HD), grads_key.reshape(TOKENS, HD), grads_value.reshape(TOKENS, HD))
    out_query, out_key, out_value = lax.map(one_head, (query_all, key_all, value_all, grad_all))
    return (out_query.transpose(1, 0, 2).reshape(TOKENS, HEADS * HD), out_key.transpose(1, 0, 2).reshape(TOKENS, HEADS * HD), out_value.transpose(1, 0, 2).reshape(TOKENS, HEADS * HD))
```

```python
import functools
import math

import jax
import jax.numpy as jnp
from jax import lax
from jax.experimental import pallas as pl
from jax.experimental.pallas import tpu as pltpu
from jax.sharding import PartitionSpec as P

HD = 128
CHUNK = 4
HALF = CHUNK // 2
MESH = pl.DeviceIdType.MESH
CORE, ROW, CHAIN, BACK = range(4)


def spikes(words_ref, head, words):
    bits = HD // words
    packed = words_ref[head * words : (head + 1) * words, :]
    shifts = lax.broadcasted_iota(jnp.int32, (words, bits, packed.shape[1]), 1)
    spread = jnp.right_shift(packed[:, None, :], shifts) & 1
    return spread.reshape(HD, packed.shape[1]).astype(jnp.float32).astype(jnp.bfloat16)


def scan_kernel(
    groups, stretches,
    query_ref, key_ref, value_hbm, grad_hbm,
    carry_hbm, heads_hbm,
    value_buf, grad_buf, carry, own, chip, core_out, core_in, row_out, row_in,
    chain_out, chain_in, back_out,
    send_sem, recv_sem, swap_send, swap_recv, local_sem, out_sem,
):
    tokens, width = value_buf.shape
    head_count = width // HD
    words = query_ref.shape[0] // head_count
    chunks = head_count // CHUNK
    part = tokens // groups
    group = lax.axis_index("head")
    place = lax.axis_index("ctx")
    core, row, plane = place % 2, (place // 2) % 2, place // 4
    planes = stretches // 4
    mate = (group, place + 1 - 2 * core)
    across = (group, place + 2 - 4 * row)
    above, below = (group, place + 4), (group, place - 4)
    has_above, has_below = plane < planes - 1, plane > 0
    partners = [(lax.rem(group + k, groups), place) for k in range(1, groups)]

    barrier = pltpu.get_barrier_semaphore()
    for device in partners + [mate, across]:
        pl.semaphore_signal(barrier, inc=1, device_id=device, device_id_type=MESH)

    @pl.when(has_above)
    def _():
        pl.semaphore_signal(barrier, inc=1, device_id=above, device_id_type=MESH)

    @pl.when(has_below)
    def _():
        pl.semaphore_signal(barrier, inc=1, device_id=below, device_id_type=MESH)

    def cols(chunk):
        return pl.ds(chunk * CHUNK * HD, CHUNK * HD)

    def grad_cols(owner, chunk):
        return pl.ds(pl.multiple_of(owner * width + chunk * CHUNK * HD, HD), CHUNK * HD)

    my_rows = pl.ds(pl.multiple_of(group * part, part), part)
    value_in = [
        pltpu.make_async_copy(value_hbm.at[:, cols(j)], value_buf.at[:, cols(j)], local_sem.at[0, j])
        for j in range(chunks)
    ]
    grad_in = [
        pltpu.make_async_copy(
            grad_hbm.at[0, :, grad_cols(group, j)], grad_buf.at[my_rows, cols(j)], local_sem.at[1, j]
        )
        for j in range(chunks)
    ]
    for copy in value_in + grad_in:
        copy.start()

    pl.semaphore_wait(
        barrier, groups + 1 + has_above.astype(jnp.int32) + has_below.astype(jnp.int32)
    )

    swaps = [
        [
            pltpu.make_async_remote_copy(
                src_ref=grad_hbm.at[0, :, grad_cols(device[0], j)],
                dst_ref=grad_buf.at[my_rows, cols(j)],
                send_sem=swap_send.at[k, j],
                recv_sem=swap_recv.at[k, j],
                device_id=device,
                device_id_type=MESH,
            )
            for k, device in enumerate(partners)
        ]
        for j in range(chunks)
    ]
    for copies in swaps:
        for copy in copies:
            copy.start()

    def remote(kind, which, j, src, dst, device):
        return pltpu.make_async_remote_copy(
            src_ref=src,
            dst_ref=dst,
            send_sem=send_sem.at[kind, which, j],
            recv_sem=recv_sem.at[kind, which, j],
            device_id=device,
            device_id_type=MESH,
        )

    def mine(j):
        return pl.ds(j * CHUNK + HALF * core, HALF)

    def core_copy(which, j):
        return remote(CORE, which, j, core_out.at[which, j], core_in.at[which, j], mate)

    def row_copy(which, j):
        return remote(ROW, which, j, row_out.at[which, j], row_in.at[which, j], across)

    def chain_copy(which, j):
        device = below if which else above
        return remote(CHAIN, which, j, chain_out.at[which, j], chain_in.at[which, j], device)

    def back_copy(which, j):
        return remote(BACK, which, j, back_out.at[which, j], carry.at[which, mine(j)], mate)

    first_core = core == 0

    def terms(which, j):
        if which == 0:
            value_in[j].wait()
        else:
            grad_in[j].wait()
            for copy in swaps[j]:
                copy.wait_recv()
        dots = []
        for head in range(j * CHUNK, (j + 1) * CHUNK):
            rows = value_buf if which == 0 else grad_buf
            spike = spikes(key_ref if which == 0 else query_ref, head, words)
            dots.append(
                jnp.dot(
                    spike, rows[:, head * HD : (head + 1) * HD], preferred_element_type=jnp.float32
                )
            )
        for i in range(HALF):
            low, high = dots[i], dots[HALF + i]
            own[which, j, i] = jnp.where(first_core, low, high)
            core_out[which, j, i] = jnp.where(first_core, high, low)
        core_copy(which, j).start()

    def chip_sum(which, j):
        core_copy(which, j).wait_recv()
        total = own[which, j] + core_in[which, j]
        chip[which, j] = total
        row_out[which, j] = total.astype(jnp.bfloat16)
        row_copy(which, j).start()

    def chain(which, j):
        starts, goes_on = (has_above, has_below) if which else (has_below, has_above)
        row_copy(which, j).wait_recv()

        @pl.when(starts)
        def _():
            chain_copy(which, j).wait_recv()

        @pl.when(jnp.logical_not(starts))
        def _():
            chain_in[which, j] = jnp.zeros_like(chain_in[which, j])

        base = chain_in[which, j].astype(jnp.float32)
        other = row_in[which, j].astype(jnp.float32)

        @pl.when(goes_on)
        def _():
            chain_out[which, j] = (base + other + chip[which, j]).astype(jnp.bfloat16)
            chain_copy(which, j).start()

        base = base + jnp.where(row == (1 - which), other, 0.0)
        nearer = first_core if which == 0 else jnp.logical_not(first_core)
        more = base + jnp.where(nearer, own[which, j], core_in[which, j])
        back_out[which, j] = jnp.where(nearer, more, base).astype(jnp.bfloat16)
        back_copy(which, j).start()
        carry[which, mine(j)] = jnp.where(nearer, base, more).astype(jnp.bfloat16)

    def carry_out(which, j):
        heads = pl.ds(j * CHUNK, CHUNK)
        return pltpu.make_async_copy(
            carry.at[which, heads], carry_hbm.at[which, heads], out_sem.at[which, j]
        )

    def heads_out(j):
        return pltpu.make_async_copy(
            grad_buf.at[:, cols(j)], heads_hbm.at[:, cols(j)], out_sem.at[2, j]
        )

    def land(which, j):
        back_copy(which, j).wait_recv()
        carry_out(which, j).start()

    for j in range(chunks + 1):
        if j < chunks:
            terms(0, j)
        if j > 0:
            chip_sum(0, j - 1)
    for j in range(chunks + 1):
        if j < chunks:
            terms(1, j)
            heads_out(j).start()
            chain(0, j)
            chip_sum(1, j)
        if j > 0:
            chain(1, j - 1)
    for which in range(2):
        for j in range(chunks):
            land(which, j)

    for j in range(chunks):
        for copy in swaps[j]:
            copy.wait_send()
        heads_out(j).wait()
        for which in range(2):
            core_copy(which, j).wait_send()
            row_copy(which, j).wait_send()
            back_copy(which, j).wait_send()

            @pl.when(has_below if which else has_above)
            def _():
                chain_copy(which, j).wait_send()

            carry_out(which, j).wait()


def grads_kernel(
    att_scale,
    tiles_ref, query_ref, key_ref, value_ref, grad_ref, state_ref, adjoint_ref,
    query_out, key_out, value_out,
):
    tokens = value_ref.shape[0]
    words = query_ref.shape[0] // CHUNK
    tile_count = tiles_ref.shape[1]
    size = tokens // tile_count
    t = lax.broadcasted_iota(jnp.int32, (tokens, tokens), 0)
    s = lax.broadcasted_iota(jnp.int32, (tokens, tokens), 1)

    def masked(t, s):
        keep = jnp.where((t >= s) & (t // size == s // size), att_scale, 0.0)
        for a in range(tile_count):
            for b in range(a):
                allowed = tiles_ref[0, a, b].astype(jnp.float32) * att_scale
                keep = jnp.where((t // size == a) & (s // size == b), allowed, keep)
        return keep

    keep, keep_t = masked(t, s), masked(s, t)

    def dot(a, b, dims=((1,), (0,))):
        return lax.dot_general(a, b, (dims, ((), ())), preferred_element_type=jnp.float32)

    last = ((1,), (1,))
    for i in range(CHUNK):
        columns = slice(i * HD, (i + 1) * HD)
        query = spikes(query_ref, i, words)
        key_t = spikes(key_ref, i, words).T
        value = value_ref[:, columns]
        grad = grad_ref[:, columns]
        weights = (dot(grad, value, last) * keep).astype(jnp.bfloat16)
        weights_t = (dot(value, grad, last) * keep_t).astype(jnp.bfloat16)
        att_t = (dot(key_t, query) * keep_t).astype(jnp.bfloat16)
        query_out[:, columns] = (
            dot(weights, key_t) + att_scale * dot(grad, state_ref[0, i], last)
        ).astype(jnp.bfloat16)
        key_out[:, columns] = (
            dot(weights_t, query, last) + att_scale * dot(value, adjoint_ref[0, i], last)
        ).astype(jnp.bfloat16)
        value_out[:, columns] = (
            dot(att_t, grad) + att_scale * dot(key_t, adjoint_ref[0, i])
        ).astype(jnp.bfloat16)


def local(query_bits, key_bits, values, grad_out, tile_mask):
    groups, stretches = lax.axis_size("head"), lax.axis_size("ctx")
    tokens, width = values.shape
    heads = width // HD
    chunks = heads // CHUNK
    att_scale = 4.0 / (HD * math.sqrt(tokens * stretches))
    bf16, f32 = jnp.bfloat16, jnp.float32
    slots = (2, chunks, HALF, HD, HD)
    vmem, any_space = pl.BlockSpec(memory_space=pltpu.VMEM), pl.BlockSpec(memory_space=pl.ANY)
    carry, grad_heads = pl.pallas_call(
        functools.partial(scan_kernel, groups, stretches),
        out_shape=(
            jax.ShapeDtypeStruct((2, heads, HD, HD), bf16),
            jax.ShapeDtypeStruct((tokens, width), bf16),
        ),
        in_specs=[vmem, vmem, any_space, any_space],
        out_specs=(any_space, any_space),
        scratch_shapes=[
            pltpu.VMEM((tokens, width), bf16),
            pltpu.VMEM((tokens, width), bf16),
            pltpu.VMEM((2, heads, HD, HD), bf16),
            pltpu.VMEM(slots, f32),
            pltpu.VMEM(slots, f32),
            pltpu.VMEM(slots, f32),
            pltpu.VMEM(slots, f32),
            pltpu.VMEM(slots, bf16),
            pltpu.VMEM(slots, bf16),
            pltpu.VMEM(slots, bf16),
            pltpu.VMEM(slots, bf16),
            pltpu.VMEM(slots, bf16),
            pltpu.SemaphoreType.DMA((4, 2, chunks)),
            pltpu.SemaphoreType.DMA((4, 2, chunks)),
            pltpu.SemaphoreType.DMA((groups - 1, chunks)),
            pltpu.SemaphoreType.DMA((groups - 1, chunks)),
            pltpu.SemaphoreType.DMA((2, chunks)),
            pltpu.SemaphoreType.DMA((3, chunks)),
        ],
        compiler_params=pltpu.CompilerParams(
            collective_id=0, has_side_effects=True, vmem_limit_bytes=32 * 1024 * 1024
        ),
    )(query_bits, key_bits, values, grad_out)

    rows = CHUNK * query_bits.shape[0] // heads
    packed = pl.BlockSpec((rows, tokens), lambda j: (j, 0))
    wide = pl.BlockSpec((tokens, CHUNK * HD), lambda j: (0, j))
    result = jax.ShapeDtypeStruct((tokens, width), bf16)
    return pl.pallas_call(
        functools.partial(grads_kernel, att_scale),
        grid=(chunks,),
        out_shape=(result, result, result),
        in_specs=[
            pl.BlockSpec(memory_space=pltpu.SMEM),
            packed,
            packed,
            wide,
            wide,
            pl.BlockSpec((1, CHUNK, HD, HD), lambda j: (0, j, 0, 0)),
            pl.BlockSpec((1, CHUNK, HD, HD), lambda j: (1, j, 0, 0)),
        ],
        out_specs=(wide, wide, wide),
        compiler_params=pltpu.CompilerParams(vmem_limit_bytes=32 * 1024 * 1024),
    )(tile_mask, query_bits, key_bits, values, grad_heads, carry, carry)


def solution(mesh):
    return jax.shard_map(
        local,
        mesh=mesh,
        in_specs=(
            P("head", "ctx"),
            P("head", "ctx"),
            P("ctx", "head"),
            P("ctx", "head", None),
            P("ctx", None, None),
        ),
        out_specs=(P("ctx", "head"), P("ctx", "head"), P("ctx", "head")),
        check_vma=False,
    )
```

```python
import functools
import math

import jax
import jax.numpy as jnp
from jax import lax
from jax.experimental import pallas as pl
from jax.experimental.pallas import tpu as pltpu
from jax.sharding import PartitionSpec as P

HD = 128
CHUNK = 2
HALF = CHUNK // 2
STEP = 4
LAG = 2
MESH = pl.DeviceIdType.MESH
CORE, ROW, CHAIN, BACK = range(4)


def spikes(words_ref, head, words):
    bits = HD // words
    packed = words_ref[head * words : (head + 1) * words, :]
    shifts = lax.broadcasted_iota(jnp.int32, (words, bits, packed.shape[1]), 1)
    spread = jnp.right_shift(packed[:, None, :], shifts) & 1
    return spread.reshape(HD, packed.shape[1]).astype(jnp.float32).astype(jnp.bfloat16)


def scan_kernel(
    groups, stretches,
    query_hbm, key_hbm, value_hbm, grad_hbm,
    carry_hbm, heads_hbm,
    query_ref, key_ref, value_buf, grad_buf, carry, own, chip, core_out, core_in, row_out, row_in,
    chain_out, chain_in, back_out,
    send_sem, recv_sem, swap_send, swap_recv, local_sem, bits_sem, out_sem,
):
    tokens, width = value_buf.shape
    head_count = width // HD
    words = query_ref.shape[0] // head_count
    chunks = head_count // CHUNK
    part = tokens // groups
    group = lax.axis_index("head")
    place = lax.axis_index("ctx")
    core, row, plane = place % 2, (place // 2) % 2, place // 4
    planes = stretches // 4
    mate = (group, place + 1 - 2 * core)
    across = (group, place + 2 - 4 * row)
    above, below = (group, place + 4), (group, place - 4)
    has_above, has_below = plane < planes - 1, plane > 0
    partners = [(lax.rem(group + k, groups), place) for k in range(1, groups)]

    barrier = pltpu.get_barrier_semaphore()
    for device in partners + [mate, across]:
        pl.semaphore_signal(barrier, inc=1, device_id=device, device_id_type=MESH)

    @pl.when(has_above)
    def _():
        pl.semaphore_signal(barrier, inc=1, device_id=above, device_id_type=MESH)

    @pl.when(has_below)
    def _():
        pl.semaphore_signal(barrier, inc=1, device_id=below, device_id_type=MESH)

    def cols(chunk):
        return pl.ds(chunk * CHUNK * HD, CHUNK * HD)

    def grad_cols(owner, chunk):
        return pl.ds(pl.multiple_of(owner * width + chunk * CHUNK * HD, HD), CHUNK * HD)

    my_rows = pl.ds(pl.multiple_of(group * part, part), part)
    value_in = [
        pltpu.make_async_copy(value_hbm.at[:, cols(j)], value_buf.at[:, cols(j)], local_sem.at[0, j])
        for j in range(chunks)
    ]
    grad_in = [
        pltpu.make_async_copy(
            grad_hbm.at[0, :, grad_cols(group, j)], grad_buf.at[my_rows, cols(j)], local_sem.at[1, j]
        )
        for j in range(chunks)
    ]
    key_in = pltpu.make_async_copy(key_hbm, key_ref, bits_sem.at[0])
    query_in = pltpu.make_async_copy(query_hbm, query_ref, bits_sem.at[1])
    for copy in [key_in] + value_in + [query_in] + grad_in:
        copy.start()

    pl.semaphore_wait(
        barrier, groups + 1 + has_above.astype(jnp.int32) + has_below.astype(jnp.int32)
    )

    swaps = [
        [
            pltpu.make_async_remote_copy(
                src_ref=grad_hbm.at[0, :, grad_cols(device[0], j)],
                dst_ref=grad_buf.at[my_rows, cols(j)],
                send_sem=swap_send.at[k, j],
                recv_sem=swap_recv.at[k, j],
                device_id=device,
                device_id_type=MESH,
            )
            for k, device in enumerate(partners)
        ]
        for j in range(chunks)
    ]
    for copies in swaps:
        for copy in copies:
            copy.start()

    def remote(kind, which, j, src, dst, device):
        return pltpu.make_async_remote_copy(
            src_ref=src,
            dst_ref=dst,
            send_sem=send_sem.at[kind, which, j],
            recv_sem=recv_sem.at[kind, which, j],
            device_id=device,
            device_id_type=MESH,
        )

    def mine(j):
        return pl.ds(j * CHUNK + HALF * core, HALF)

    def core_copy(which, j):
        return remote(CORE, which, j, core_out.at[which, j], core_in.at[which, j], mate)

    def row_copy(which, j):
        return remote(ROW, which, j, row_out.at[which, j], row_in.at[which, j], across)

    def chain_copy(which, j):
        device = below if which else above
        return remote(CHAIN, which, j, chain_out.at[which, j], chain_in.at[which, j], device)

    def back_copy(which, j):
        return remote(BACK, which, j, back_out.at[which, j], carry.at[which, mine(j)], mate)

    first_core = core == 0

    def terms(which, j):
        if which == 0:
            value_in[j].wait()
        else:
            grad_in[j].wait()
            for copy in swaps[j]:
                copy.wait_recv()
        dots = []
        for head in range(j * CHUNK, (j + 1) * CHUNK):
            rows = value_buf if which == 0 else grad_buf
            spike = spikes(key_ref if which == 0 else query_ref, head, words)
            dots.append(
                jnp.dot(
                    spike, rows[:, head * HD : (head + 1) * HD], preferred_element_type=jnp.float32
                )
            )
        for i in range(HALF):
            low, high = dots[i], dots[HALF + i]
            own[which, j, i] = jnp.where(first_core, low, high)
            core_out[which, j, i] = jnp.where(first_core, high, low)
        core_copy(which, j).start()

    def chip_sum(which, j):
        core_copy(which, j).wait_recv()
        total = own[which, j] + core_in[which, j]
        chip[which, j] = total
        row_out[which, j] = total.astype(jnp.bfloat16)
        row_copy(which, j).start()

    def chain(which, j):
        starts, goes_on = (has_above, has_below) if which else (has_below, has_above)
        row_copy(which, j).wait_recv()

        @pl.when(starts)
        def _():
            chain_copy(which, j).wait_recv()

        @pl.when(jnp.logical_not(starts))
        def _():
            chain_in[which, j] = jnp.zeros_like(chain_in[which, j])

        base = chain_in[which, j].astype(jnp.float32)
        other = row_in[which, j].astype(jnp.float32)

        @pl.when(goes_on)
        def _():
            chain_out[which, j] = (base + other + chip[which, j]).astype(jnp.bfloat16)
            chain_copy(which, j).start()

        base = base + jnp.where(row == (1 - which), other, 0.0)
        nearer = first_core if which == 0 else jnp.logical_not(first_core)
        more = base + jnp.where(nearer, own[which, j], core_in[which, j])
        back_out[which, j] = jnp.where(nearer, more, base).astype(jnp.bfloat16)
        back_copy(which, j).start()
        carry[which, mine(j)] = jnp.where(nearer, base, more).astype(jnp.bfloat16)

    def carry_out(which, j):
        heads = pl.ds(j * CHUNK, CHUNK)
        return pltpu.make_async_copy(
            carry.at[which, heads], carry_hbm.at[which, heads], out_sem.at[which, j]
        )

    def heads_out(j):
        return pltpu.make_async_copy(
            grad_buf.at[:, cols(j)], heads_hbm.at[:, cols(j)], out_sem.at[2, j]
        )

    def land(which, j):
        back_copy(which, j).wait_recv()
        carry_out(which, j).start()

    def chain_slot(which, j):
        @pl.when((j >= 0) & (j < chunks))
        def _():
            chain(which, j)

    key_in.wait()
    for j in range(chunks + 1):
        if j < chunks:
            terms(0, j)
        if j > 0:
            chip_sum(0, j - 1)
    query_in.wait()
    for slot in range(LAG + chunks + planes - 1):
        if slot < chunks:
            terms(1, slot)
            heads_out(slot).start()
        if slot < chunks + planes - 1:
            chain_slot(0, slot - plane)
        if 0 < slot <= chunks:
            chip_sum(1, slot - 1)
        if slot >= LAG:
            chain_slot(1, slot - LAG - (planes - 1 - plane))
    for which in range(2):
        for j in range(chunks):
            land(which, j)

    for j in range(chunks):
        for copy in swaps[j]:
            copy.wait_send()
        heads_out(j).wait()
        for which in range(2):
            core_copy(which, j).wait_send()
            row_copy(which, j).wait_send()
            back_copy(which, j).wait_send()

            @pl.when(has_below if which else has_above)
            def _():
                chain_copy(which, j).wait_send()

            carry_out(which, j).wait()


def grads_kernel(
    att_scale,
    tiles_ref, query_ref, key_ref, value_ref, grad_ref, state_ref, adjoint_ref,
    query_out, key_out, value_out,
):
    tokens = value_ref.shape[0]
    words = query_ref.shape[0] // STEP
    tile_count = tiles_ref.shape[1]
    size = tokens // tile_count
    t = lax.broadcasted_iota(jnp.int32, (tokens, tokens), 0)
    s = lax.broadcasted_iota(jnp.int32, (tokens, tokens), 1)

    def masked(t, s):
        keep = jnp.where((t >= s) & (t // size == s // size), att_scale, 0.0)
        for a in range(tile_count):
            for b in range(a):
                allowed = tiles_ref[0, a, b].astype(jnp.float32) * att_scale
                keep = jnp.where((t // size == a) & (s // size == b), allowed, keep)
        return keep

    keep, keep_t = masked(t, s), masked(s, t)

    def dot(a, b, dims=((1,), (0,))):
        return lax.dot_general(a, b, (dims, ((), ())), preferred_element_type=jnp.float32)

    last = ((1,), (1,))
    for i in range(STEP):
        columns = slice(i * HD, (i + 1) * HD)
        query = spikes(query_ref, i, words)
        key_t = spikes(key_ref, i, words).T
        value = value_ref[:, columns]
        grad = grad_ref[:, columns]
        weights = (dot(grad, value, last) * keep).astype(jnp.bfloat16)
        weights_t = (dot(value, grad, last) * keep_t).astype(jnp.bfloat16)
        att_t = (dot(key_t, query) * keep_t).astype(jnp.bfloat16)
        query_out[:, columns] = (
            dot(weights, key_t) + att_scale * dot(grad, state_ref[0, i], last)
        ).astype(jnp.bfloat16)
        key_out[:, columns] = (
            dot(weights_t, query, last) + att_scale * dot(value, adjoint_ref[0, i], last)
        ).astype(jnp.bfloat16)
        value_out[:, columns] = (
            dot(att_t, grad) + att_scale * dot(key_t, adjoint_ref[0, i])
        ).astype(jnp.bfloat16)


def local(query_bits, key_bits, values, grad_out, tile_mask):
    groups, stretches = lax.axis_size("head"), lax.axis_size("ctx")
    tokens, width = values.shape
    heads = width // HD
    chunks = heads // CHUNK
    att_scale = 4.0 / (HD * math.sqrt(tokens * stretches))
    bf16, f32 = jnp.bfloat16, jnp.float32
    slots = (2, chunks, HALF, HD, HD)
    hbm = pl.BlockSpec(memory_space=pltpu.HBM)
    carry, grad_heads = pl.pallas_call(
        functools.partial(scan_kernel, groups, stretches),
        out_shape=(
            jax.ShapeDtypeStruct((2, heads, HD, HD), bf16),
            jax.ShapeDtypeStruct((tokens, width), bf16),
        ),
        in_specs=[hbm, hbm, hbm, hbm],
        out_specs=(hbm, hbm),
        scratch_shapes=[
            pltpu.VMEM(query_bits.shape, jnp.int32),
            pltpu.VMEM(key_bits.shape, jnp.int32),
            pltpu.VMEM((tokens, width), bf16),
            pltpu.VMEM((tokens, width), bf16),
            pltpu.VMEM((2, heads, HD, HD), bf16),
            pltpu.VMEM(slots, f32),
            pltpu.VMEM(slots, f32),
            pltpu.VMEM(slots, f32),
            pltpu.VMEM(slots, f32),
            pltpu.VMEM(slots, bf16),
            pltpu.VMEM(slots, bf16),
            pltpu.VMEM(slots, bf16),
            pltpu.VMEM(slots, bf16),
            pltpu.VMEM(slots, bf16),
            pltpu.SemaphoreType.DMA((4, 2, chunks)),
            pltpu.SemaphoreType.DMA((4, 2, chunks)),
            pltpu.SemaphoreType.DMA((groups - 1, chunks)),
            pltpu.SemaphoreType.DMA((groups - 1, chunks)),
            pltpu.SemaphoreType.DMA((2, chunks)),
            pltpu.SemaphoreType.DMA((2,)),
            pltpu.SemaphoreType.DMA((3, chunks)),
        ],
        compiler_params=pltpu.CompilerParams(
            collective_id=0, has_side_effects=True, vmem_limit_bytes=63 * 1024 * 1024
        ),
    )(query_bits, key_bits, values, grad_out)

    rows = STEP * query_bits.shape[0] // heads
    packed = pl.BlockSpec((rows, tokens), lambda j: (j, 0))
    wide = pl.BlockSpec((tokens, STEP * HD), lambda j: (0, j))
    result = jax.ShapeDtypeStruct((tokens, width), bf16)
    return pl.pallas_call(
        functools.partial(grads_kernel, att_scale),
        grid=(heads // STEP,),
        out_shape=(result, result, result),
        in_specs=[
            pl.BlockSpec(memory_space=pltpu.SMEM),
            packed,
            packed,
            wide,
            wide,
            pl.BlockSpec((1, STEP, HD, HD), lambda j: (0, j, 0, 0)),
            pl.BlockSpec((1, STEP, HD, HD), lambda j: (1, j, 0, 0)),
        ],
        out_specs=(wide, wide, wide),
        compiler_params=pltpu.CompilerParams(vmem_limit_bytes=63 * 1024 * 1024),
    )(tile_mask, query_bits, key_bits, values, grad_heads, carry, carry)


def solution(mesh):
    return jax.shard_map(
        local,
        mesh=mesh,
        in_specs=(
            P("head", "ctx"),
            P("head", "ctx"),
            P("ctx", "head"),
            P("ctx", "head", None),
            P("ctx", None, None),
        ),
        out_specs=(P("ctx", "head"), P("ctx", "head"), P("ctx", "head")),
        check_vma=False,
    )
```

```python
import functools
import math

import jax
import jax.numpy as jnp
from jax import lax
from jax.experimental import pallas as pl
from jax.experimental.pallas import tpu as pltpu
from jax.sharding import PartitionSpec as P

HD = 128
CHUNK = 2
HALF = CHUNK // 2
LAG = 1
MESH = pl.DeviceIdType.MESH
CORE, ROW, CHAIN, BACK = range(4)


def spikes(words_ref, head, words):
    bits = HD // words
    packed = words_ref[head * words : (head + 1) * words, :]
    shifts = lax.broadcasted_iota(jnp.int32, (words, bits, packed.shape[1]), 1)
    spread = jnp.right_shift(packed[:, None, :], shifts) & 1
    return spread.reshape(HD, packed.shape[1]).astype(jnp.float32).astype(jnp.bfloat16)


def scan_kernel(
    groups, stretches, att_scale,
    tiles_ref, query_hbm, key_hbm, value_hbm, grad_hbm,
    query_out, key_out, value_out,
    query_ref, key_ref, query_spk, key_spk, key_rows, keep, keep_t,
    query_part, key_part, value_part, query_buf, key_buf, result_buf, value_buf, grad_buf, carry, own, chip, core_out, core_in, row_out, row_in,
    chain_out, chain_in, back_out,
    send_sem, recv_sem, swap_send, swap_recv, local_sem, bits_sem, out_sem,
):
    tokens, width = value_buf.shape
    head_count = width // HD
    words = query_ref.shape[0] // head_count
    chunks = head_count // CHUNK
    part = tokens // groups
    group = lax.axis_index("head")
    place = lax.axis_index("ctx")
    core, row, plane = place % 2, (place // 2) % 2, place // 4
    planes = stretches // 4
    mate = (group, place + 1 - 2 * core)
    across = (group, place + 2 - 4 * row)
    above, below = (group, place + 4), (group, place - 4)
    has_above, has_below = plane < planes - 1, plane > 0
    partners = [(lax.rem(group + k, groups), place) for k in range(1, groups)]

    barrier = pltpu.get_barrier_semaphore()
    for device in partners + [mate, across]:
        pl.semaphore_signal(barrier, inc=1, device_id=device, device_id_type=MESH)

    @pl.when(has_above)
    def _():
        pl.semaphore_signal(barrier, inc=1, device_id=above, device_id_type=MESH)

    @pl.when(has_below)
    def _():
        pl.semaphore_signal(barrier, inc=1, device_id=below, device_id_type=MESH)

    def cols(chunk):
        return pl.ds(chunk * CHUNK * HD, CHUNK * HD)

    def grad_cols(owner, chunk):
        return pl.ds(pl.multiple_of(owner * width + chunk * CHUNK * HD, HD), CHUNK * HD)

    my_rows = pl.ds(pl.multiple_of(group * part, part), part)
    value_in = [
        pltpu.make_async_copy(value_hbm.at[:, cols(j)], value_buf.at[:, cols(j)], local_sem.at[0, j])
        for j in range(chunks)
    ]
    grad_in = [
        pltpu.make_async_copy(
            grad_hbm.at[0, :, grad_cols(group, j)], grad_buf.at[my_rows, cols(j)], local_sem.at[1, j]
        )
        for j in range(chunks)
    ]
    key_in = pltpu.make_async_copy(key_hbm, key_ref, bits_sem.at[0])
    query_in = pltpu.make_async_copy(query_hbm, query_ref, bits_sem.at[1])
    for copy in [key_in] + value_in + [query_in] + grad_in:
        copy.start()

    tile_count = tiles_ref.shape[1]
    size = tokens // tile_count
    down = lax.broadcasted_iota(jnp.int32, (tokens, tokens), 0)
    along = lax.broadcasted_iota(jnp.int32, (tokens, tokens), 1)

    def masked(t, s):
        mask = jnp.where((t >= s) & (t // size == s // size), att_scale, 0.0)
        for later in range(tile_count):
            for earlier in range(later):
                allowed = tiles_ref[0, later, earlier].astype(jnp.float32) * att_scale
                mask = jnp.where((t // size == later) & (s // size == earlier), allowed, mask)
        return mask

    keep[...] = masked(down, along)
    keep_t[...] = masked(along, down)
    key_in.wait()
    for head in range(head_count):
        key_spk[head] = spikes(key_ref, head, words)

    pl.semaphore_wait(
        barrier, groups + 1 + has_above.astype(jnp.int32) + has_below.astype(jnp.int32)
    )

    swaps = [
        [
            pltpu.make_async_remote_copy(
                src_ref=grad_hbm.at[0, :, grad_cols(device[0], j)],
                dst_ref=grad_buf.at[my_rows, cols(j)],
                send_sem=swap_send.at[k, j],
                recv_sem=swap_recv.at[k, j],
                device_id=device,
                device_id_type=MESH,
            )
            for k, device in enumerate(partners)
        ]
        for j in range(chunks)
    ]
    for copies in swaps:
        for copy in copies:
            copy.start()

    def remote(kind, which, j, src, dst, device):
        return pltpu.make_async_remote_copy(
            src_ref=src,
            dst_ref=dst,
            send_sem=send_sem.at[kind, which, j],
            recv_sem=recv_sem.at[kind, which, j],
            device_id=device,
            device_id_type=MESH,
        )

    def mine(j):
        return pl.ds(j * CHUNK + HALF * core, HALF)

    def core_copy(which, j):
        return remote(CORE, which, j, core_out.at[which, j], core_in.at[which, j], mate)

    def row_copy(which, j):
        return remote(ROW, which, j, row_out.at[which, j], row_in.at[which, j], across)

    def chain_copy(which, j):
        device = below if which else above
        return remote(CHAIN, which, j, chain_out.at[which, j], chain_in.at[which, j], device)

    def back_copy(which, j):
        return remote(BACK, which, j, back_out.at[which, j], carry.at[which, mine(j)], mate)

    first_core = core == 0

    def terms(which, j):
        if which == 0:
            value_in[j].wait()
        else:
            grad_in[j].wait()
            for copy in swaps[j]:
                copy.wait_recv()
        dots = []
        for head in range(j * CHUNK, (j + 1) * CHUNK):
            rows = value_buf if which == 0 else grad_buf
            spike = key_spk if which == 0 else query_spk
            dots.append(
                jnp.dot(
                    spike[head], rows[:, head * HD : (head + 1) * HD], preferred_element_type=jnp.float32
                )
            )
        for i in range(HALF):
            low, high = dots[i], dots[HALF + i]
            own[which, j, i] = jnp.where(first_core, low, high)
            core_out[which, j, i] = jnp.where(first_core, high, low)
        core_copy(which, j).start()

    def chip_sum(which, j):
        core_copy(which, j).wait_recv()
        total = own[which, j] + core_in[which, j]
        chip[which, j] = total
        row_out[which, j] = total.astype(jnp.bfloat16)
        row_copy(which, j).start()

    def chain(which, j):
        starts, goes_on = (has_above, has_below) if which else (has_below, has_above)
        row_copy(which, j).wait_recv()

        @pl.when(starts)
        def _():
            chain_copy(which, j).wait_recv()

        @pl.when(jnp.logical_not(starts))
        def _():
            chain_in[which, j] = jnp.zeros_like(chain_in[which, j])

        base = chain_in[which, j].astype(jnp.float32)
        other = row_in[which, j].astype(jnp.float32)

        @pl.when(goes_on)
        def _():
            chain_out[which, j] = (base + other + chip[which, j]).astype(jnp.bfloat16)
            chain_copy(which, j).start()

        base = base + jnp.where(row == (1 - which), other, 0.0)
        nearer = first_core if which == 0 else jnp.logical_not(first_core)
        more = base + jnp.where(nearer, own[which, j], core_in[which, j])
        back_out[which, j] = jnp.where(nearer, more, base).astype(jnp.bfloat16)
        back_copy(which, j).start()
        carry[which, mine(j)] = jnp.where(nearer, base, more).astype(jnp.bfloat16)

    def dot(x, y, dims=((1,), (0,))):
        return lax.dot_general(x, y, (dims, ((), ())), preferred_element_type=jnp.float32)

    last = ((1,), (1,))

    def lanes(head):
        return slice(head * HD, (head + 1) * HD)

    def heads_of(j):
        return range(j * CHUNK, (j + 1) * CHUNK)

    def within(j):
        for head in heads_of(j):
            query = query_spk[head]
            rows = key_rows[head]
            value = value_buf[:, lanes(head)]
            grad = grad_buf[:, lanes(head)]
            weights = (dot(grad, value, last) * keep[...]).astype(jnp.bfloat16)
            query_part[:, lanes(head)] = dot(weights, rows)
            weights_t = (dot(value, grad, last) * keep_t[...]).astype(jnp.bfloat16)
            key_part[:, lanes(head)] = dot(weights_t, query, last)
            att_t = (dot(rows, query) * keep_t[...]).astype(jnp.bfloat16)
            value_part[:, lanes(head)] = dot(att_t, grad)

    def result_copy(kind, j):
        source = (query_buf, key_buf, result_buf)[kind]
        target = (query_out, key_out, value_out)[kind]
        return pltpu.make_async_copy(
            source.at[:, cols(j)], target.at[:, cols(j)], out_sem.at[kind, j]
        )

    def finish_query(j):
        back_copy(0, j).wait_recv()
        for head in heads_of(j):
            across_part = dot(grad_buf[:, lanes(head)], carry[0, head], last)
            query_buf[:, lanes(head)] = (
                query_part[:, lanes(head)] + att_scale * across_part
            ).astype(jnp.bfloat16)
        result_copy(0, j).start()

    def finish_key_value(j):
        back_copy(1, j).wait_recv()
        for head in heads_of(j):
            adjoint = carry[1, head]
            key_buf[:, lanes(head)] = (
                key_part[:, lanes(head)]
                + att_scale * dot(value_buf[:, lanes(head)], adjoint, last)
            ).astype(jnp.bfloat16)
            result_buf[:, lanes(head)] = (
                value_part[:, lanes(head)] + att_scale * dot(key_rows[head], adjoint)
            ).astype(jnp.bfloat16)
        result_copy(1, j).start()
        result_copy(2, j).start()

    def chain_slot(which, j):
        @pl.when((j >= 0) & (j < chunks))
        def _():
            chain(which, j)

    for j in range(chunks + 1):
        if j < chunks:
            terms(0, j)
        if j > 0:
            chip_sum(0, j - 1)
    query_in.wait()
    for head in range(head_count):
        query_spk[head] = spikes(query_ref, head, words)
        key_rows[head] = key_spk[head].T

    state_slots = chunks + planes - 1
    asked = 0
    done = 0
    for slot in range(LAG + chunks + planes):
        if slot < chunks:
            terms(1, slot)
        ahead = min(2 * slot + 2, state_slots) if slot < chunks else state_slots
        for early in range(asked, ahead):
            chain_slot(0, early - plane)
        asked = ahead
        if 0 < slot <= chunks:
            within(slot - 1)
        if slot < chunks:
            chip_sum(1, slot)
        if LAG <= slot < LAG + state_slots:
            chain_slot(1, slot - LAG - (planes - 1 - plane))
        ready = min(max(asked - planes, 0), slot, chunks)
        for j in range(done, ready):
            finish_query(j)
        done = ready
        if slot >= LAG + planes:
            finish_key_value(slot - LAG - planes)
    for j in range(done, chunks):
        finish_query(j)

    for j in range(chunks):
        for copy in swaps[j]:
            copy.wait_send()
        for which in range(2):
            core_copy(which, j).wait_send()
            row_copy(which, j).wait_send()
            back_copy(which, j).wait_send()

            @pl.when(has_below if which else has_above)
            def _():
                chain_copy(which, j).wait_send()

        for kind in range(3):
            result_copy(kind, j).wait()


def local(query_bits, key_bits, values, grad_out, tile_mask):
    groups, stretches = lax.axis_size("head"), lax.axis_size("ctx")
    tokens, width = values.shape
    heads = width // HD
    chunks = heads // CHUNK
    att_scale = 4.0 / (HD * math.sqrt(tokens * stretches))
    bf16, f32 = jnp.bfloat16, jnp.float32
    slots = (2, chunks, HALF, HD, HD)
    hbm = pl.BlockSpec(memory_space=pltpu.HBM)
    spk, wide = (heads, HD, tokens), (tokens, width)
    result = jax.ShapeDtypeStruct(wide, bf16)
    return pl.pallas_call(
        functools.partial(scan_kernel, groups, stretches, att_scale),
        out_shape=(result, result, result),
        in_specs=[pl.BlockSpec(memory_space=pltpu.SMEM), hbm, hbm, hbm, hbm],
        out_specs=(hbm, hbm, hbm),
        scratch_shapes=[
            pltpu.VMEM(query_bits.shape, jnp.int32),
            pltpu.VMEM(key_bits.shape, jnp.int32),
            pltpu.VMEM(spk, bf16),
            pltpu.VMEM(spk, bf16),
            pltpu.VMEM((heads, tokens, HD), bf16),
            pltpu.VMEM((tokens, tokens), f32),
            pltpu.VMEM((tokens, tokens), f32),
            pltpu.VMEM(wide, f32),
            pltpu.VMEM(wide, f32),
            pltpu.VMEM(wide, f32),
            pltpu.VMEM(wide, bf16),
            pltpu.VMEM(wide, bf16),
            pltpu.VMEM(wide, bf16),
            pltpu.VMEM((tokens, width), bf16),
            pltpu.VMEM((tokens, width), bf16),
            pltpu.VMEM((2, heads, HD, HD), bf16),
            pltpu.VMEM(slots, f32),
            pltpu.VMEM(slots, f32),
            pltpu.VMEM(slots, f32),
            pltpu.VMEM(slots, f32),
            pltpu.VMEM(slots, bf16),
            pltpu.VMEM(slots, bf16),
            pltpu.VMEM(slots, bf16),
            pltpu.VMEM(slots, bf16),
            pltpu.VMEM(slots, bf16),
            pltpu.SemaphoreType.DMA((4, 2, chunks)),
            pltpu.SemaphoreType.DMA((4, 2, chunks)),
            pltpu.SemaphoreType.DMA((groups - 1, chunks)),
            pltpu.SemaphoreType.DMA((groups - 1, chunks)),
            pltpu.SemaphoreType.DMA((2, chunks)),
            pltpu.SemaphoreType.DMA((2,)),
            pltpu.SemaphoreType.DMA((3, chunks)),
        ],
        compiler_params=pltpu.CompilerParams(
            collective_id=0, has_side_effects=True, vmem_limit_bytes=63 * 1024 * 1024
        ),
    )(tile_mask, query_bits, key_bits, values, grad_out)


def solution(mesh):
    return jax.shard_map(
        local,
        mesh=mesh,
        in_specs=(
            P("head", "ctx"),
            P("head", "ctx"),
            P("ctx", "head"),
            P("ctx", "head", None),
            P("ctx", None, None),
        ),
        out_specs=(P("ctx", "head"), P("ctx", "head"), P("ctx", "head")),
        check_vma=False,
    )
```

```python
import functools
import math

import jax
import jax.numpy as jnp
from jax import lax
from jax.experimental import pallas as pl
from jax.experimental.pallas import tpu as pltpu
from jax.sharding import PartitionSpec as P

HD = 128
CHUNK = 2
HALF = CHUNK // 2
LAG = 3
SKEW = 2
STATE_SKEW = 4
PIECES = 4
MESH = pl.DeviceIdType.MESH
CORE, ROW, CHAIN, BACK = range(4)


def spikes(words_ref, head, words):
    bits = HD // words
    packed = words_ref[head * words : (head + 1) * words, :]
    shifts = lax.broadcasted_iota(jnp.int32, (words, bits, packed.shape[1]), 1)
    spread = jnp.right_shift(packed[:, None, :], shifts) & 1
    return spread.reshape(HD, packed.shape[1]).astype(jnp.float32).astype(jnp.bfloat16)


def scan_kernel(
    groups, stretches, att_scale,
    tiles_ref, query_hbm, key_hbm, value_hbm, grad_hbm,
    query_out, key_out, value_out,
    query_ref, key_ref, query_spk, key_spk, key_rows, keep, keep_t,
    query_part, key_part, value_part, query_buf, key_buf, result_buf, value_buf, grad_buf, carry, own, chip, core_out, core_in, row_out, row_in,
    chain_out, chain_in, back_out,
    send_sem, recv_sem, swap_send, swap_recv, local_sem, bits_sem, out_sem,
):
    tokens, width = value_buf.shape
    head_count = width // HD
    words = query_ref.shape[0] // head_count
    chunks = head_count // CHUNK
    part = tokens // groups
    group = lax.axis_index("head")
    place = lax.axis_index("ctx")
    core, row, plane = place % 2, (place // 2) % 2, place // 4
    planes = stretches // 4
    mate = (group, place + 1 - 2 * core)
    across = (group, place + 2 - 4 * row)
    above, below = (group, place + 4), (group, place - 4)
    has_above, has_below = plane < planes - 1, plane > 0
    partners = [(lax.rem(group + k, groups), place) for k in range(1, groups)]

    barrier = pltpu.get_barrier_semaphore()
    for device in partners + [mate, across]:
        pl.semaphore_signal(barrier, inc=1, device_id=device, device_id_type=MESH)

    @pl.when(has_above)
    def _():
        pl.semaphore_signal(barrier, inc=1, device_id=above, device_id_type=MESH)

    @pl.when(has_below)
    def _():
        pl.semaphore_signal(barrier, inc=1, device_id=below, device_id_type=MESH)

    def cols(chunk):
        return pl.ds(chunk * CHUNK * HD, CHUNK * HD)

    def grad_cols(owner, chunk):
        return pl.ds(pl.multiple_of(owner * width + chunk * CHUNK * HD, HD), CHUNK * HD)

    my_rows = pl.ds(pl.multiple_of(group * part, part), part)
    value_in = [
        pltpu.make_async_copy(value_hbm.at[:, cols(j)], value_buf.at[:, cols(j)], local_sem.at[0, j])
        for j in range(chunks)
    ]
    grad_in = [
        pltpu.make_async_copy(
            grad_hbm.at[0, :, grad_cols(group, j)], grad_buf.at[my_rows, cols(j)], local_sem.at[1, j]
        )
        for j in range(chunks)
    ]
    key_in = pltpu.make_async_copy(key_hbm, key_ref, bits_sem.at[0])
    query_in = pltpu.make_async_copy(query_hbm, query_ref, bits_sem.at[1])
    for copy in [key_in] + value_in + [query_in] + grad_in:
        copy.start()

    tile_count = tiles_ref.shape[1]
    size = tokens // tile_count
    down = lax.broadcasted_iota(jnp.int32, (tokens, tokens), 0)
    along = lax.broadcasted_iota(jnp.int32, (tokens, tokens), 1)

    def masked(t, s):
        mask = jnp.where((t >= s) & (t // size == s // size), att_scale, 0.0)
        for later in range(tile_count):
            for earlier in range(later):
                allowed = tiles_ref[0, later, earlier].astype(jnp.float32) * att_scale
                mask = jnp.where((t // size == later) & (s // size == earlier), allowed, mask)
        return mask

    keep[...] = masked(down, along)
    keep_t[...] = masked(along, down)
    key_in.wait()
    for head in range(head_count):
        key_spk[head] = spikes(key_ref, head, words)

    pl.semaphore_wait(
        barrier, groups + 1 + has_above.astype(jnp.int32) + has_below.astype(jnp.int32)
    )

    swaps = [
        [
            pltpu.make_async_remote_copy(
                src_ref=grad_hbm.at[0, :, grad_cols(device[0], j)],
                dst_ref=grad_buf.at[my_rows, cols(j)],
                send_sem=swap_send.at[k, j],
                recv_sem=swap_recv.at[k, j],
                device_id=device,
                device_id_type=MESH,
            )
            for k, device in enumerate(partners)
        ]
        for j in range(chunks)
    ]
    for copies in swaps:
        for copy in copies:
            copy.start()

    def remote(kind, which, j, src, dst, device):
        return pltpu.make_async_remote_copy(
            src_ref=src,
            dst_ref=dst,
            send_sem=send_sem.at[kind, which, j],
            recv_sem=recv_sem.at[kind, which, j],
            device_id=device,
            device_id_type=MESH,
        )

    def mine(j):
        return pl.ds(j * CHUNK + HALF * core, HALF)

    def core_copy(which, j):
        return remote(CORE, which, j, core_out.at[which, j], core_in.at[which, j], mate)

    def row_copy(which, j):
        return remote(ROW, which, j, row_out.at[which, j], row_in.at[which, j], across)

    def chain_copy(which, j):
        device = below if which else above
        return remote(CHAIN, which, j, chain_out.at[which, j], chain_in.at[which, j], device)

    def back_copy(which, j):
        return remote(BACK, which, j, back_out.at[which, j], carry.at[which, mine(j)], mate)

    first_core = core == 0

    def terms(which, j):
        if which == 0:
            value_in[j].wait()
        else:
            grad_in[j].wait()
            for copy in swaps[j]:
                copy.wait_recv()
        dots = []
        for head in range(j * CHUNK, (j + 1) * CHUNK):
            rows = value_buf if which == 0 else grad_buf
            spike = key_spk if which == 0 else query_spk
            dots.append(
                jnp.dot(
                    spike[head], rows[:, head * HD : (head + 1) * HD], preferred_element_type=jnp.float32
                )
            )
        for i in range(HALF):
            low, high = dots[i], dots[HALF + i]
            own[which, j, i] = jnp.where(first_core, low, high)
            core_out[which, j, i] = jnp.where(first_core, high, low)
        core_copy(which, j).start()

    def chip_sum(which, j):
        core_copy(which, j).wait_recv()
        total = own[which, j] + core_in[which, j]
        chip[which, j] = total
        row_out[which, j] = total.astype(jnp.bfloat16)
        row_copy(which, j).start()

    def chain(which, j):
        starts, goes_on = (has_above, has_below) if which else (has_below, has_above)
        row_copy(which, j).wait_recv()

        @pl.when(starts)
        def _():
            chain_copy(which, j).wait_recv()

        @pl.when(jnp.logical_not(starts))
        def _():
            chain_in[which, j] = jnp.zeros_like(chain_in[which, j])

        base = chain_in[which, j].astype(jnp.float32)
        other = row_in[which, j].astype(jnp.float32)

        @pl.when(goes_on)
        def _():
            chain_out[which, j] = (base + other + chip[which, j]).astype(jnp.bfloat16)
            chain_copy(which, j).start()

        base = base + jnp.where(row == (1 - which), other, 0.0)
        nearer = first_core if which == 0 else jnp.logical_not(first_core)
        more = base + jnp.where(nearer, own[which, j], core_in[which, j])
        back_out[which, j] = jnp.where(nearer, more, base).astype(jnp.bfloat16)
        back_copy(which, j).start()
        carry[which, mine(j)] = jnp.where(nearer, base, more).astype(jnp.bfloat16)

    def dot(x, y, dims=((1,), (0,))):
        return lax.dot_general(x, y, (dims, ((), ())), preferred_element_type=jnp.float32)

    last = ((1,), (1,))

    def lanes(head):
        return slice(head * HD, (head + 1) * HD)

    def heads_of(j):
        return range(j * CHUNK, (j + 1) * CHUNK)

    def within(j):
        for head in heads_of(j):
            query = query_spk[head]
            rows = key_rows[head]
            value = value_buf[:, lanes(head)]
            grad = grad_buf[:, lanes(head)]
            weights = (dot(grad, value, last) * keep[...]).astype(jnp.bfloat16)
            query_part[:, lanes(head)] = dot(weights, rows)
            weights_t = (dot(value, grad, last) * keep_t[...]).astype(jnp.bfloat16)
            key_part[:, lanes(head)] = dot(weights_t, query, last)
            att_t = (dot(rows, query) * keep_t[...]).astype(jnp.bfloat16)
            value_part[:, lanes(head)] = dot(att_t, grad)

    def result_copy(kind, j):
        source = (query_buf, key_buf, result_buf)[kind]
        target = (query_out, key_out, value_out)[kind]
        return pltpu.make_async_copy(
            source.at[:, cols(j)], target.at[:, cols(j)], out_sem.at[kind, j]
        )

    def finish_query(j):
        back_copy(0, j).wait_recv()
        for head in heads_of(j):
            across_part = dot(grad_buf[:, lanes(head)], carry[0, head], last)
            query_buf[:, lanes(head)] = (
                query_part[:, lanes(head)] + att_scale * across_part
            ).astype(jnp.bfloat16)
        result_copy(0, j).start()

    def finish_key_value(j):
        back_copy(1, j).wait_recv()
        for head in heads_of(j):
            adjoint = carry[1, head]
            key_buf[:, lanes(head)] = (
                key_part[:, lanes(head)]
                + att_scale * dot(value_buf[:, lanes(head)], adjoint, last)
            ).astype(jnp.bfloat16)
            result_buf[:, lanes(head)] = (
                value_part[:, lanes(head)] + att_scale * dot(key_rows[head], adjoint)
            ).astype(jnp.bfloat16)
        result_copy(1, j).start()
        result_copy(2, j).start()

    def chain_slot(which, j):
        @pl.when((j >= 0) & (j < chunks))
        def _():
            chain(which, j)

    for j in range(chunks):
        terms(0, j)
    query_in.wait()
    for head in range(head_count):
        query_spk[head] = spikes(query_ref, head, words)
        key_rows[head] = key_spk[head].T
    for j in range(chunks):
        chip_sum(0, j)

    span = planes - 1
    state_slots = chunks + STATE_SKEW * span
    slots = LAG + chunks + SKEW * span
    asked = done = 0
    for slot in range(slots + 2):
        if slot < chunks:
            terms(1, slot)
        ahead = min(2 * slot, state_slots)
        for early in range(asked, ahead):
            chain_slot(0, early - STATE_SKEW * plane)
        asked = ahead
        if 0 < slot <= chunks:
            chip_sum(1, slot - 1)
        if LAG <= slot < slots:
            chain_slot(1, slot - LAG - SKEW * (span - plane))
        if 0 < slot <= chunks:
            within(slot - 1)
        ready = min(max(asked - STATE_SKEW * span - 2, 0), slot, chunks)
        for j in range(done, ready):
            finish_query(j)
        done = max(done, ready)
        if slot >= slots + 2 - chunks:
            finish_key_value(slot - (slots + 2 - chunks))
    for early in range(asked, state_slots):
        chain_slot(0, early - STATE_SKEW * plane)
    for j in range(done, chunks):
        finish_query(j)

    for j in range(chunks):
        for copy in swaps[j]:
            copy.wait_send()
        for which in range(2):
            core_copy(which, j).wait_send()
            row_copy(which, j).wait_send()
            back_copy(which, j).wait_send()

            @pl.when(has_below if which else has_above)
            def _():
                chain_copy(which, j).wait_send()

        for kind in range(3):
            result_copy(kind, j).wait()


def place_kernel(query_in, key_in, value_in, query_out, key_out, value_out, held, sem):
    rows = held.shape[1] // PIECES
    inward, outward = [], []
    for kind, (source, target) in enumerate(
        ((query_in, query_out), (key_in, key_out), (value_in, value_out))
    ):
        for piece in range(PIECES):
            part = pl.ds(piece * rows, rows)
            inward.append(
                pltpu.make_async_copy(source.at[part], held.at[kind, part], sem.at[0, kind, piece])
            )
            outward.append(
                pltpu.make_async_copy(held.at[kind, part], target.at[part], sem.at[1, kind, piece])
            )
    for copy in inward:
        copy.start()
    for arrived, leaving in zip(inward, outward):
        arrived.wait()
        leaving.start()
    for copy in outward:
        copy.wait()


def local(query_bits, key_bits, values, grad_out, tile_mask):
    groups, stretches = lax.axis_size("head"), lax.axis_size("ctx")
    tokens, width = values.shape
    heads = width // HD
    chunks = heads // CHUNK
    att_scale = 4.0 / (HD * math.sqrt(tokens * stretches))
    bf16, f32 = jnp.bfloat16, jnp.float32
    slots = (2, chunks, HALF, HD, HD)
    hbm = pl.BlockSpec(memory_space=pltpu.HBM)
    spk, wide = (heads, HD, tokens), (tokens, width)
    result = jax.ShapeDtypeStruct(wide, bf16)
    results = pl.pallas_call(
        functools.partial(scan_kernel, groups, stretches, att_scale),
        out_shape=(result, result, result),
        in_specs=[pl.BlockSpec(memory_space=pltpu.SMEM), hbm, hbm, hbm, hbm],
        out_specs=(hbm, hbm, hbm),
        scratch_shapes=[
            pltpu.VMEM(query_bits.shape, jnp.int32),
            pltpu.VMEM(key_bits.shape, jnp.int32),
            pltpu.VMEM(spk, bf16),
            pltpu.VMEM(spk, bf16),
            pltpu.VMEM((heads, tokens, HD), bf16),
            pltpu.VMEM((tokens, tokens), f32),
            pltpu.VMEM((tokens, tokens), f32),
            pltpu.VMEM(wide, f32),
            pltpu.VMEM(wide, f32),
            pltpu.VMEM(wide, f32),
            pltpu.VMEM(wide, bf16),
            pltpu.VMEM(wide, bf16),
            pltpu.VMEM(wide, bf16),
            pltpu.VMEM((tokens, width), bf16),
            pltpu.VMEM((tokens, width), bf16),
            pltpu.VMEM((2, heads, HD, HD), bf16),
            pltpu.VMEM(slots, f32),
            pltpu.VMEM(slots, f32),
            pltpu.VMEM(slots, f32),
            pltpu.VMEM(slots, f32),
            pltpu.VMEM(slots, bf16),
            pltpu.VMEM(slots, bf16),
            pltpu.VMEM(slots, bf16),
            pltpu.VMEM(slots, bf16),
            pltpu.VMEM(slots, bf16),
            pltpu.SemaphoreType.DMA((4, 2, chunks)),
            pltpu.SemaphoreType.DMA((4, 2, chunks)),
            pltpu.SemaphoreType.DMA((groups - 1, chunks)),
            pltpu.SemaphoreType.DMA((groups - 1, chunks)),
            pltpu.SemaphoreType.DMA((2, chunks)),
            pltpu.SemaphoreType.DMA((2,)),
            pltpu.SemaphoreType.DMA((3, chunks)),
        ],
        compiler_params=pltpu.CompilerParams(
            collective_id=0, has_side_effects=True, vmem_limit_bytes=63 * 1024 * 1024
        ),
    )(tile_mask, query_bits, key_bits, values, grad_out)
    return pl.pallas_call(
        place_kernel,
        out_shape=(result, result, result),
        in_specs=[hbm, hbm, hbm],
        out_specs=(hbm, hbm, hbm),
        scratch_shapes=[
            pltpu.VMEM((3, *wide), bf16),
            pltpu.SemaphoreType.DMA((2, 3, PIECES)),
        ],
        compiler_params=pltpu.CompilerParams(vmem_limit_bytes=63 * 1024 * 1024),
    )(*results)


def solution(mesh):
    return jax.shard_map(
        local,
        mesh=mesh,
        in_specs=(
            P("head", "ctx"),
            P("head", "ctx"),
            P("ctx", "head"),
            P("ctx", "head", None),
            P("ctx", None, None),
        ),
        out_specs=(P("ctx", "head"), P("ctx", "head"), P("ctx", "head")),
        check_vma=False,
    )
```

```python
import functools
import math

import jax
import jax.numpy as jnp
from jax import lax
from jax.experimental import pallas as pl
from jax.experimental.pallas import tpu as pltpu
from jax.sharding import PartitionSpec as P

HD = 128
CHUNK = 2
HALF = CHUNK // 2
LAG = 3
SKEW = 2
STATE_SKEW = 4
PIECES = 4
MESH = pl.DeviceIdType.MESH
CORE, ROW, CHAIN, BACK = range(4)


def spikes(words_ref, head, words):
    bits = HD // words
    packed = words_ref[head * words : (head + 1) * words, :]
    shifts = lax.broadcasted_iota(jnp.int32, (words, bits, packed.shape[1]), 1)
    spread = jnp.right_shift(packed[:, None, :], shifts) & 1
    return spread.reshape(HD, packed.shape[1]).astype(jnp.float32).astype(jnp.bfloat16)


def scan_kernel(
    groups, stretches, att_scale,
    tiles_ref, query_hbm, key_hbm, value_hbm, grad_hbm,
    query_out, key_out, value_out,
    query_ref, key_ref, query_spk, key_spk, key_rows, keep, keep_t,
    query_part, key_part, value_part, query_buf, key_buf, result_buf, value_buf, grad_buf, carry, own, chip, core_out, core_in, row_out, row_in,
    chain_out, chain_in, back_out,
    send_sem, recv_sem, swap_send, swap_recv, local_sem, bits_sem, out_sem,
):
    tokens, width = value_buf.shape
    head_count = width // HD
    words = query_ref.shape[0] // head_count
    chunks = head_count // CHUNK
    part = tokens // groups
    group = lax.axis_index("head")
    place = lax.axis_index("ctx")
    core, row, plane = place % 2, (place // 2) % 2, place // 4
    planes = stretches // 4
    mate = (group, place + 1 - 2 * core)
    across = (group, place + 2 - 4 * row)
    above, below = (group, place + 4), (group, place - 4)
    has_above, has_below = plane < planes - 1, plane > 0
    partners = [(lax.rem(group + k, groups), place) for k in range(1, groups)]

    barrier = pltpu.get_barrier_semaphore()
    for device in partners + [mate, across]:
        pl.semaphore_signal(barrier, inc=1, device_id=device, device_id_type=MESH)

    @pl.when(has_above)
    def _():
        pl.semaphore_signal(barrier, inc=1, device_id=above, device_id_type=MESH)

    @pl.when(has_below)
    def _():
        pl.semaphore_signal(barrier, inc=1, device_id=below, device_id_type=MESH)

    def cols(chunk):
        return pl.ds(chunk * CHUNK * HD, CHUNK * HD)

    def grad_cols(owner, chunk):
        return pl.ds(pl.multiple_of(owner * width + chunk * CHUNK * HD, HD), CHUNK * HD)

    my_rows = pl.ds(pl.multiple_of(group * part, part), part)
    value_in = [
        pltpu.make_async_copy(value_hbm.at[:, cols(j)], value_buf.at[:, cols(j)], local_sem.at[0, j])
        for j in range(chunks)
    ]
    grad_in = [
        pltpu.make_async_copy(
            grad_hbm.at[0, :, grad_cols(group, j)], grad_buf.at[my_rows, cols(j)], local_sem.at[1, j]
        )
        for j in range(chunks)
    ]
    key_in = pltpu.make_async_copy(key_hbm, key_ref, bits_sem.at[0])
    query_in = pltpu.make_async_copy(query_hbm, query_ref, bits_sem.at[1])
    for copy in [key_in] + value_in + [query_in] + grad_in:
        copy.start()

    pl.semaphore_wait(
        barrier, groups + 1 + has_above.astype(jnp.int32) + has_below.astype(jnp.int32)
    )

    swaps = [
        [
            pltpu.make_async_remote_copy(
                src_ref=grad_hbm.at[0, :, grad_cols(device[0], j)],
                dst_ref=grad_buf.at[my_rows, cols(j)],
                send_sem=swap_send.at[k, j],
                recv_sem=swap_recv.at[k, j],
                device_id=device,
                device_id_type=MESH,
            )
            for k, device in enumerate(partners)
        ]
        for j in range(chunks)
    ]
    for copies in swaps:
        for copy in copies:
            copy.start()

    tile_count = tiles_ref.shape[1]
    size = tokens // tile_count
    down = lax.broadcasted_iota(jnp.int32, (tokens, tokens), 0)
    along = lax.broadcasted_iota(jnp.int32, (tokens, tokens), 1)

    def masked(t, s):
        mask = jnp.where((t >= s) & (t // size == s // size), att_scale, 0.0)
        for later in range(tile_count):
            for earlier in range(later):
                allowed = tiles_ref[0, later, earlier].astype(jnp.float32) * att_scale
                mask = jnp.where((t // size == later) & (s // size == earlier), allowed, mask)
        return mask

    keep[...] = masked(down, along)
    keep_t[...] = masked(along, down)
    key_in.wait()
    for head in range(head_count):
        key_spk[head] = spikes(key_ref, head, words)

    def remote(kind, which, j, src, dst, device):
        return pltpu.make_async_remote_copy(
            src_ref=src,
            dst_ref=dst,
            send_sem=send_sem.at[kind, which, j],
            recv_sem=recv_sem.at[kind, which, j],
            device_id=device,
            device_id_type=MESH,
        )

    def mine(j):
        return pl.ds(j * CHUNK + HALF * core, HALF)

    def core_copy(which, j):
        return remote(CORE, which, j, core_out.at[which, j], core_in.at[which, j], mate)

    def row_copy(which, j):
        return remote(ROW, which, j, row_out.at[which, j], row_in.at[which, j], across)

    def chain_copy(which, j):
        device = below if which else above
        return remote(CHAIN, which, j, chain_out.at[which, j], chain_in.at[which, j], device)

    def back_copy(which, j):
        return remote(BACK, which, j, back_out.at[which, j], carry.at[which, mine(j)], mate)

    first_core = core == 0

    def terms(which, j):
        if which == 0:
            value_in[j].wait()
        else:
            grad_in[j].wait()
            for copy in swaps[j]:
                copy.wait_recv()
        dots = []
        for head in range(j * CHUNK, (j + 1) * CHUNK):
            rows = value_buf if which == 0 else grad_buf
            spike = key_spk if which == 0 else query_spk
            dots.append(
                jnp.dot(
                    spike[head], rows[:, head * HD : (head + 1) * HD], preferred_element_type=jnp.float32
                )
            )
        for i in range(HALF):
            low, high = dots[i], dots[HALF + i]
            own[which, j, i] = jnp.where(first_core, low, high)
            core_out[which, j, i] = jnp.where(first_core, high, low)
        core_copy(which, j).start()

    def chip_sum(which, j):
        core_copy(which, j).wait_recv()
        total = own[which, j] + core_in[which, j]
        chip[which, j] = total
        row_out[which, j] = total.astype(jnp.bfloat16)
        row_copy(which, j).start()

    def chain(which, j):
        starts, goes_on = (has_above, has_below) if which else (has_below, has_above)
        row_copy(which, j).wait_recv()

        @pl.when(starts)
        def _():
            chain_copy(which, j).wait_recv()

        @pl.when(jnp.logical_not(starts))
        def _():
            chain_in[which, j] = jnp.zeros_like(chain_in[which, j])

        base = chain_in[which, j].astype(jnp.float32)
        other = row_in[which, j].astype(jnp.float32)

        @pl.when(goes_on)
        def _():
            chain_out[which, j] = (base + other + chip[which, j]).astype(jnp.bfloat16)
            chain_copy(which, j).start()

        base = base + jnp.where(row == (1 - which), other, 0.0)
        nearer = first_core if which == 0 else jnp.logical_not(first_core)
        more = base + jnp.where(nearer, own[which, j], core_in[which, j])
        back_out[which, j] = jnp.where(nearer, more, base).astype(jnp.bfloat16)
        back_copy(which, j).start()
        carry[which, mine(j)] = jnp.where(nearer, base, more).astype(jnp.bfloat16)

    def dot(x, y, dims=((1,), (0,))):
        return lax.dot_general(x, y, (dims, ((), ())), preferred_element_type=jnp.float32)

    last = ((1,), (1,))

    def lanes(head):
        return slice(head * HD, (head + 1) * HD)

    def heads_of(j):
        return range(j * CHUNK, (j + 1) * CHUNK)

    def within(j):
        for head in heads_of(j):
            query = query_spk[head]
            rows = key_rows[head]
            value = value_buf[:, lanes(head)]
            grad = grad_buf[:, lanes(head)]
            weights = (dot(grad, value, last) * keep[...]).astype(jnp.bfloat16)
            query_part[:, lanes(head)] = dot(weights, rows)
            weights_t = (dot(value, grad, last) * keep_t[...]).astype(jnp.bfloat16)
            key_part[:, lanes(head)] = dot(weights_t, query, last)
            att_t = (dot(rows, query) * keep_t[...]).astype(jnp.bfloat16)
            value_part[:, lanes(head)] = dot(att_t, grad)

    def result_copy(kind, j):
        source = (query_buf, key_buf, result_buf)[kind]
        target = (query_out, key_out, value_out)[kind]
        return pltpu.make_async_copy(
            source.at[:, cols(j)], target.at[:, cols(j)], out_sem.at[kind, j]
        )

    def finish_query(j):
        back_copy(0, j).wait_recv()
        for head in heads_of(j):
            across_part = dot(grad_buf[:, lanes(head)], carry[0, head], last)
            query_buf[:, lanes(head)] = (
                query_part[:, lanes(head)] + att_scale * across_part
            ).astype(jnp.bfloat16)
        result_copy(0, j).start()

    def finish_key_value(j):
        back_copy(1, j).wait_recv()
        for head in heads_of(j):
            adjoint = carry[1, head]
            key_buf[:, lanes(head)] = (
                key_part[:, lanes(head)]
                + att_scale * dot(value_buf[:, lanes(head)], adjoint, last)
            ).astype(jnp.bfloat16)
            result_buf[:, lanes(head)] = (
                value_part[:, lanes(head)] + att_scale * dot(key_rows[head], adjoint)
            ).astype(jnp.bfloat16)
        result_copy(1, j).start()
        result_copy(2, j).start()

    def chain_slot(which, j):
        @pl.when((j >= 0) & (j < chunks))
        def _():
            chain(which, j)

    for j in range(chunks):
        terms(0, j)
    query_in.wait()
    for head in range(head_count):
        query_spk[head] = spikes(query_ref, head, words)
        key_rows[head] = key_spk[head].T
    for j in range(chunks):
        chip_sum(0, j)

    span = planes - 1
    state_slots = chunks + STATE_SKEW * span
    slots = LAG + chunks + SKEW * span
    asked = done = 0
    for slot in range(slots + 2):
        if slot < chunks:
            terms(1, slot)
        ahead = min(2 * slot, state_slots)
        for early in range(asked, ahead):
            chain_slot(0, early - STATE_SKEW * plane)
        asked = ahead
        if 0 < slot <= chunks:
            chip_sum(1, slot - 1)
        if LAG <= slot < slots:
            chain_slot(1, slot - LAG - SKEW * (span - plane))
        if 0 < slot <= chunks:
            within(slot - 1)
        ready = min(max(asked - STATE_SKEW * span - 2, 0), slot, chunks)
        for j in range(done, ready):
            finish_query(j)
        done = max(done, ready)
        if slot >= slots + 2 - chunks:
            finish_key_value(slot - (slots + 2 - chunks))
    for early in range(asked, state_slots):
        chain_slot(0, early - STATE_SKEW * plane)
    for j in range(done, chunks):
        finish_query(j)

    for j in range(chunks):
        for copy in swaps[j]:
            copy.wait_send()
        for which in range(2):
            core_copy(which, j).wait_send()
            row_copy(which, j).wait_send()
            back_copy(which, j).wait_send()

            @pl.when(has_below if which else has_above)
            def _():
                chain_copy(which, j).wait_send()

        for kind in range(3):
            result_copy(kind, j).wait()


def place_kernel(query_in, key_in, value_in, query_out, key_out, value_out, held, sem):
    rows = held.shape[1] // PIECES
    inward, outward = [], []
    for kind, (source, target) in enumerate(
        ((query_in, query_out), (key_in, key_out), (value_in, value_out))
    ):
        for piece in range(PIECES):
            part = pl.ds(piece * rows, rows)
            inward.append(
                pltpu.make_async_copy(source.at[part], held.at[kind, part], sem.at[0, kind, piece])
            )
            outward.append(
                pltpu.make_async_copy(held.at[kind, part], target.at[part], sem.at[1, kind, piece])
            )
    for copy in inward:
        copy.start()
    for arrived, leaving in zip(inward, outward):
        arrived.wait()
        leaving.start()
    for copy in outward:
        copy.wait()


def local(query_bits, key_bits, values, grad_out, tile_mask):
    groups, stretches = lax.axis_size("head"), lax.axis_size("ctx")
    tokens, width = values.shape
    heads = width // HD
    chunks = heads // CHUNK
    att_scale = 4.0 / (HD * math.sqrt(tokens * stretches))
    bf16, f32 = jnp.bfloat16, jnp.float32
    slots = (2, chunks, HALF, HD, HD)
    hbm = pl.BlockSpec(memory_space=pltpu.HBM)
    spk, wide = (heads, HD, tokens), (tokens, width)
    result = jax.ShapeDtypeStruct(wide, bf16)
    results = pl.pallas_call(
        functools.partial(scan_kernel, groups, stretches, att_scale),
        out_shape=(result, result, result),
        in_specs=[pl.BlockSpec(memory_space=pltpu.SMEM), hbm, hbm, hbm, hbm],
        out_specs=(hbm, hbm, hbm),
        scratch_shapes=[
            pltpu.VMEM(query_bits.shape, jnp.int32),
            pltpu.VMEM(key_bits.shape, jnp.int32),
            pltpu.VMEM(spk, bf16),
            pltpu.VMEM(spk, bf16),
            pltpu.VMEM((heads, tokens, HD), bf16),
            pltpu.VMEM((tokens, tokens), f32),
            pltpu.VMEM((tokens, tokens), f32),
            pltpu.VMEM(wide, f32),
            pltpu.VMEM(wide, f32),
            pltpu.VMEM(wide, f32),
            pltpu.VMEM(wide, bf16),
            pltpu.VMEM(wide, bf16),
            pltpu.VMEM(wide, bf16),
            pltpu.VMEM((tokens, width), bf16),
            pltpu.VMEM((tokens, width), bf16),
            pltpu.VMEM((2, heads, HD, HD), bf16),
            pltpu.VMEM(slots, f32),
            pltpu.VMEM(slots, f32),
            pltpu.VMEM(slots, f32),
            pltpu.VMEM(slots, f32),
            pltpu.VMEM(slots, bf16),
            pltpu.VMEM(slots, bf16),
            pltpu.VMEM(slots, bf16),
            pltpu.VMEM(slots, bf16),
            pltpu.VMEM(slots, bf16),
            pltpu.SemaphoreType.DMA((4, 2, chunks)),
            pltpu.SemaphoreType.DMA((4, 2, chunks)),
            pltpu.SemaphoreType.DMA((groups - 1, chunks)),
            pltpu.SemaphoreType.DMA((groups - 1, chunks)),
            pltpu.SemaphoreType.DMA((2, chunks)),
            pltpu.SemaphoreType.DMA((2,)),
            pltpu.SemaphoreType.DMA((3, chunks)),
        ],
        compiler_params=pltpu.CompilerParams(
            collective_id=0, has_side_effects=True, vmem_limit_bytes=63 * 1024 * 1024
        ),
    )(tile_mask, query_bits, key_bits, values, grad_out)
    return pl.pallas_call(
        place_kernel,
        out_shape=(result, result, result),
        in_specs=[hbm, hbm, hbm],
        out_specs=(hbm, hbm, hbm),
        scratch_shapes=[
            pltpu.VMEM((3, *wide), bf16),
            pltpu.SemaphoreType.DMA((2, 3, PIECES)),
        ],
        compiler_params=pltpu.CompilerParams(vmem_limit_bytes=63 * 1024 * 1024),
    )(*results)


def solution(mesh):
    return jax.shard_map(
        local,
        mesh=mesh,
        in_specs=(
            P("head", "ctx"),
            P("head", "ctx"),
            P("ctx", "head"),
            P("ctx", "head", None),
            P("ctx", None, None),
        ),
        out_specs=(P("ctx", "head"), P("ctx", "head"), P("ctx", "head")),
        check_vma=False,
    )
```
